32 devices in a mesh: groups: 2 (over y), rows: 4 (over x, core), cols: 4 (over z).
Axes of the slice: x: 2, y: 2, z: 4, core: 2. Of those that a mesh axis runs over, the one named last changes fastest.
Arguments:
- source_emb: bfloat16 [8192, 256], P(('groups', 'rows', 'cols')), parts along dimension 0, may hold values from -400 to 400
- target_emb: bfloat16 [8192, 256], P(('groups', 'cols', 'rows')), parts along dimension 0, may hold values from -400 to 400
- source_mass: float32 [8192], P(('groups', 'rows', 'cols')), parts along dimension 0, may hold values from 0.25 to 4
- target_mass: float32 [8192], P(('groups', 'cols', 'rows')), parts along dimension 0, may hold values from 0.25 to 4
- cand_cols: int32 [64, 16], P(('groups', 'rows'), 'cols'), parts along dimension 0, may hold values from 0 to 7, as said below
- cand_count: int32 [64, 4], P(('groups', 'rows'), 'cols'), parts along dimension 0, may hold values from 1 to 4, as said below
Outputs:
- source_potential: float32 [8192], P(('groups', 'rows', 'cols')), parts along dimension 0
- target_potential: float32 [8192], P(('groups', 'cols', 'rows')), parts along dimension 0
The draws below stay inside these ranges and needn't reach their ends.
There are 2 independent parts, one for each index of `groups`. The reference program is written for one: setup_inputs(seed, part) draws one part's arguments, and reference() takes and returns one part's arrays. A program takes and returns all parts, laid end to end along the dimension named above; each array names one. Nothing has to cross between parts.
Inputs may be any that keep to these rules, and one draw needn't show every extreme that they name: `cand_cols`: entries c * 4 to c * 4 + 3 of row s are distinct local numbers of target blocks of column group c; only the first cand_count[s, c] of them are pairs. Within each row group and column group, the first entries of every 8 consecutive source blocks name each of the group's 8 target blocks once. `cand_count`: in every row group and column group some source block has 4 candidate blocks.
All inputs are finite; a program needn't handle non-finite values.
Results may differ from the reference program's by a relative error of at most 0.0024.
Values may be sent and summed in bfloat16 or wider, within the bound.
A program may use at most 64 MiB of HBM per device.

```python
import math
import jax
import jax.numpy as jnp
from jax import lax

W = 256
BS = 128
MOST_CANDIDATES = 4
ITERS = 2
SOURCE_ROW_BLOCKS = 8
TARGET_COL_BLOCKS = 8
SBLK = 32
NS = 4096
NT = 4096
N_ROWS = 4
N_COLS = 4


def scale_rows(base, row_key, col_key, count):
    row_scale = jnp.exp(jax.random.uniform(row_key, (count, 1)) * math.log(10.0))
    col_scale = jnp.exp(jax.random.uniform(col_key, (1, W)) * math.log(10.0))
    return (jnp.clip(base, -4.0, 4.0) * row_scale * col_scale).astype(jnp.bfloat16)


def draw_source_emb(key, part):
    key = jax.random.fold_in(key, 1)
    base_key, row_key, col_key = jax.random.split(key, 3)
    base = jax.random.normal(base_key, (NS, W))
    return scale_rows(base, row_key, col_key, NS)


def draw_target_emb(key, part):
    key = jax.random.fold_in(key, 2)
    base_key, row_key, col_key = jax.random.split(key, 3)
    base = jax.random.normal(base_key, (NT, W))
    return scale_rows(base, row_key, col_key, NT)


def draw_cand_cols(key, part):
    key = jax.random.fold_in(key, 5)
    first_key, order_key = jax.random.split(key)

    def shuffled(one_key):
        return jax.random.permutation(one_key, TARGET_COL_BLOCKS)
    tile_perm = jax.vmap(shuffled)(jax.random.split(first_key, N_ROWS * N_COLS)).reshape(N_ROWS, N_COLS, TARGET_COL_BLOCKS)
    slot_position = jnp.arange(SOURCE_ROW_BLOCKS, dtype=jnp.int32) % TARGET_COL_BLOCKS
    first = jnp.transpose(tile_perm[:, :, slot_position], (0, 2, 1)).reshape(SBLK, N_COLS)
    row_perm = jax.vmap(shuffled)(jax.random.split(order_key, SBLK * N_COLS)).reshape(SBLK, N_COLS, TARGET_COL_BLOCKS)
    leading = row_perm[:, :, :1]
    swapped = jnp.where(row_perm == first[:, :, None], leading, row_perm)
    swapped = swapped.at[:, :, 0].set(first)
    return swapped[:, :, :MOST_CANDIDATES].reshape(SBLK, N_COLS * MOST_CANDIDATES).astype(jnp.int32)


def draw_cand_count(key, part):
    key = jax.random.fold_in(key, 7)
    top_key, unscaled_key, complete_key = jax.random.split(key, 3)
    tile_top = jax.random.randint(top_key, (N_ROWS, 1, N_COLS), 1, MOST_CANDIDATES + 1)
    unscaled_values = jax.random.randint(unscaled_key, (N_ROWS, SOURCE_ROW_BLOCKS, N_COLS), 0, 65536)
    count_table = 1 + unscaled_values % tile_top
    complete_row = jax.random.randint(complete_key, (N_ROWS, 1, N_COLS), 0, SOURCE_ROW_BLOCKS)
    count_table = jnp.where(jnp.arange(SOURCE_ROW_BLOCKS, dtype=jnp.int32)[None, :, None] == complete_row, MOST_CANDIDATES, count_table)
    return count_table.reshape(SBLK, N_COLS).astype(jnp.int32)


def level_of(key, extent, shards, low, high):
    level = 1.0
    for axis_at, parts in shards:
        draws = jax.random.uniform(jax.random.fold_in(jax.random.fold_in(key, 6), axis_at), (parts,), jnp.float32, low / len(shards), high / len(shards))
        level = level * jnp.repeat(jnp.exp(draws), extent[axis_at] // parts).reshape((-1,) + (1,) * (len(extent) - 1 - axis_at))
    return level


def setup_inputs(seed: int = 0, part: int = 0) -> dict:
    key_of = jax.random.split(jax.random.key(seed), 7)
    own_keys = jax.random.split(jax.random.fold_in(key_of[6], part), 7)
    source_emb = draw_source_emb(jax.random.fold_in(jax.random.fold_in(key_of[6], part), 71), part)
    target_emb = draw_target_emb(jax.random.fold_in(jax.random.fold_in(key_of[6], part), 71), part)
    source_mass = jnp.clip(jnp.exp(math.log(4.0) - 2.7725887 * jax.random.uniform(own_keys[2], (NS,), jnp.float32) ** level_of(own_keys[2], (NS,), ((0, 16),), -0.2, 0.2)), 0.25, 4.0)
    target_mass = jnp.clip(jnp.exp(math.log(4.0) - 2.7725887 * jax.random.uniform(own_keys[3], (NT,), jnp.float32) ** level_of(own_keys[3], (NT,), ((0, 16),), -0.2, 0.2)), 0.25, 4.0)
    cand_cols = draw_cand_cols(jax.random.fold_in(jax.random.fold_in(key_of[6], part), 71), part)
    cand_count = draw_cand_count(jax.random.fold_in(jax.random.fold_in(key_of[6], part), 71), part)
    return dict(source_emb=source_emb, target_emb=target_emb, source_mass=source_mass, target_mass=target_mass, cand_cols=cand_cols, cand_count=cand_count)


regularizer_strength = 0.05

def normalize(embed):
    values = embed.astype(jnp.float32)
    factor = lax.rsqrt(lax.optimization_barrier(jnp.sum(values * values, axis=-1, keepdims=True)) + 1e-06)
    return (values * factor).astype(jnp.bfloat16)

def reference(source_emb, target_emb, source_mass, target_mass, cand_cols, cand_count):
    source_unit = normalize(source_emb).reshape(SBLK, BS, W)
    target_unit = normalize(target_emb).reshape(SBLK, BS, W)
    slot_width = N_COLS * MOST_CANDIDATES
    slot_index = jnp.arange(slot_width, dtype=jnp.int32)
    offsets = slot_index // MOST_CANDIDATES * TARGET_COL_BLOCKS
    targets_all = cand_cols + offsets[None, :]
    nonzero_pattern = slot_index[None, :] % MOST_CANDIDATES < jnp.repeat(cand_count, MOST_CANDIDATES, axis=1)

    def kernel_for(source_block):
        source_tile = source_unit[source_block].astype(jnp.float32)
        target_tiles = target_unit[targets_all[source_block]].astype(jnp.float32)
        similarity_matrix = jnp.einsum('aw,kbw->kab', source_tile, target_tiles)
        gibbs_factors = nonzero_pattern[source_block].astype(jnp.float32)
        return jnp.exp(similarity_matrix / regularizer_strength) * gibbs_factors[:, None, None]

    def row_pass(right_dual_multiplier):

        def per_block(source_block):
            kernel = kernel_for(source_block)
            return jnp.einsum('kab,kb->a', kernel, right_dual_multiplier[targets_all[source_block]], precision=lax.Precision.HIGHEST)
        return lax.map(per_block, jnp.arange(SBLK, dtype=jnp.int32))

    def col_pass(left_dual_multiplier):

        def per_block(totals, source_block):
            kernel = kernel_for(source_block)
            partial_sums = jnp.einsum('kab,a->kb', kernel, left_dual_multiplier[source_block], precision=lax.Precision.HIGHEST)
            return (totals.at[targets_all[source_block]].add(partial_sums), None)
        totals, unused = lax.scan(per_block, jnp.zeros((SBLK, BS), jnp.float32), jnp.arange(SBLK, dtype=jnp.int32))
        return totals
    mass_rows = source_mass.reshape(SBLK, BS)
    mass_cols = target_mass.reshape(SBLK, BS)
    right_dual_multiplier = jnp.ones((SBLK, BS), jnp.float32)
    left_dual_multiplier = jnp.ones((SBLK, BS), jnp.float32)
    for sweep in range(ITERS):
        left_dual_multiplier = mass_rows / row_pass(right_dual_multiplier)
        right_dual_multiplier = mass_cols / col_pass(left_dual_multiplier)
    return ((regularizer_strength * jnp.log(left_dual_multiplier)).reshape(-1), (regularizer_strength * jnp.log(right_dual_multiplier)).reshape(-1))
```

```python
import functools
import math

import jax
import jax.numpy as jnp
from jax import lax
from jax.experimental import pallas as pl
from jax.experimental.pallas import tpu as pltpu
from jax.sharding import PartitionSpec as P

BS = 128
ITERS = 2
strength = 0.05
MESH = pl.DeviceIdType.MESH
NT = (((1,), (1,)), ((), ()))
NN = (((1,), (0,)), ((), ()))


def normalize(embed):
    values = embed.astype(jnp.float32)
    factor = lax.rsqrt(jnp.sum(values * values, axis=-1, keepdims=True) + 1e-06)
    return (values * factor).astype(jnp.bfloat16)


def split_rows(vector):
    high = vector.astype(jnp.bfloat16).astype(jnp.float32)
    row = lax.broadcasted_iota(jnp.int32, (16, vector.shape[1]), 0)
    rows = jnp.where(row == 0, high, jnp.where(row == 1, vector - high, 0.0))
    return rows.astype(jnp.bfloat16)


def kernel(
    n_r, n_c,
    src_ref, tgt_ref, smass_ref, tmass_ref, cand_ref, count_ref,
    spot_ref, tpot_ref,
    sp, tp, sm, tm, mask, gibbs, rbuf, cbuf,
    s_send, s_recv, t_send, t_recv, sm_send, sm_recv, tm_send, tm_recv,
    r_send, r_recv, c_send, c_recv,
):
    me_r, me_c = lax.axis_index("rows"), lax.axis_index("cols")
    m = src_ref.shape[0]
    mb = m // BS
    S, T = n_c * m, n_r * m
    slots = cand_ref.shape[1]

    def to_col(k):
        return lax.rem(me_c + k, n_c)

    def to_row(k):
        return lax.rem(me_r + k, n_r)

    barrier = pltpu.get_barrier_semaphore()
    for k in range(1, n_c):
        pl.semaphore_signal(barrier, inc=1, device_id={"cols": to_col(k)}, device_id_type=MESH)
    for k in range(1, n_r):
        pl.semaphore_signal(barrier, inc=1, device_id={"rows": to_row(k)}, device_id_type=MESH)

    sp[me_c] = normalize(src_ref[...])
    tp[me_r] = normalize(tgt_ref[...])
    sm[me_c] = smass_ref[...]
    tm[me_r] = tmass_ref[...]
    pl.semaphore_wait(barrier, n_c + n_r - 2)

    def col_copy(ref, send, recv, k):
        return pltpu.make_async_remote_copy(
            ref, ref, send, recv, device_id={"cols": to_col(k)}, device_id_type=MESH)

    def row_copy(ref, send, recv, k):
        return pltpu.make_async_remote_copy(
            ref, ref, send, recv, device_id={"rows": to_row(k)}, device_id_type=MESH)

    s_out = [col_copy(sp.at[me_c], s_send.at[k - 1], s_recv.at[k - 1], k) for k in range(1, n_c)]
    t_out = [row_copy(tp.at[me_r], t_send.at[k - 1], t_recv.at[k - 1], k) for k in range(1, n_r)]
    sm_out = [col_copy(sm.at[me_c], sm_send.at[k - 1], sm_recv.at[k - 1], k) for k in range(1, n_c)]
    tm_out = [row_copy(tm.at[me_r], tm_send.at[k - 1], tm_recv.at[k - 1], k) for k in range(1, n_r)]
    for copy in t_out + s_out + sm_out + tm_out:
        copy.start()

    def from_col(ref_of, send, recv, k):
        owner = lax.rem(me_c + n_c - k, n_c)
        col_copy(ref_of(owner), send, recv, k).wait_recv()

    def from_row(ref_of, send, recv, k):
        owner = lax.rem(me_r + n_r - k, n_r)
        row_copy(ref_of(owner), send, recv, k).wait_recv()

    target_block = lax.broadcasted_iota(jnp.int32, mask.shape, 1) // BS
    hit = jnp.zeros(mask.shape, jnp.float32)
    for k in range(slots):
        live = (cand_ref[:, k:k + 1] == target_block) & (count_ref[...] > k)
        hit = jnp.where(live, 1.0, hit)
    mask[...] = hit

    for k in range(1, n_r):
        from_row(lambda o: tp.at[o], t_send.at[k - 1], t_recv.at[k - 1], k)

    ones = jnp.ones((16, T), jnp.bfloat16)
    width = min(T, 1024)
    scale = math.log2(math.e) / strength

    def build(owner):
        for b in range(mb):
            block = sp[owner, b * BS:(b + 1) * BS, :]
            row0 = pl.multiple_of(owner * m + b * BS, BS)
            for t0 in range(0, n_r):
                sim = lax.dot_general(block, tp[t0], NT, preferred_element_type=jnp.float32)
                live = mask[pl.ds(owner * mb + b, 1), t0 * m:(t0 + 1) * m]
                gibbs[pl.ds(row0, BS), t0 * m:(t0 + 1) * m] = (
                    jnp.exp2(sim * scale) * live).astype(jnp.bfloat16)
        rows = pl.ds(pl.multiple_of(owner * m, m), m)
        total = lax.dot_general(ones, gibbs[rows, :], NT, preferred_element_type=jnp.float32)
        rbuf[0, me_c, :, rows] = total[:1]

    build(me_c)
    for k in range(1, n_c):
        from_col(lambda o: sp.at[o], s_send.at[k - 1], s_recv.at[k - 1], k)
        build(lax.rem(me_c + n_c - k, n_c))

    def chunked(extent):
        step = min(extent, 1024)
        return [slice(i, i + step) for i in range(0, extent, step)]

    def exchange_rows(it):
        out = [col_copy(rbuf.at[it, me_c], r_send.at[it, k - 1], r_recv.at[it, k - 1], k)
               for k in range(1, n_c)]
        for copy in out:
            copy.start()
        if it == 0:
            for k in range(1, n_c):
                from_col(lambda o: sm.at[o], sm_send.at[k - 1], sm_recv.at[k - 1], k)
        for k in range(1, n_c):
            from_col(lambda o: rbuf.at[it, o], r_send.at[it, k - 1], r_recv.at[it, k - 1], k)
        total = rbuf[it, 0]
        for j in range(1, n_c):
            total = total + rbuf[it, j]
        return out, jnp.concatenate([sm[j] for j in range(n_c)], axis=1) / total

    def exchange_cols(it):
        out = [row_copy(cbuf.at[it, me_r], c_send.at[it, k - 1], c_recv.at[it, k - 1], k)
               for k in range(1, n_r)]
        for copy in out:
            copy.start()
        if it == 0:
            for k in range(1, n_r):
                from_row(lambda o: tm.at[o], tm_send.at[k - 1], tm_recv.at[k - 1], k)
        for k in range(1, n_r):
            from_row(lambda o: cbuf.at[it, o], c_send.at[it, k - 1], c_recv.at[it, k - 1], k)
        total = cbuf[it, 0]
        for j in range(1, n_r):
            total = total + cbuf[it, j]
        return out, jnp.concatenate([tm[j] for j in range(n_r)], axis=1) / total

    pending = s_out + t_out + sm_out + tm_out
    for it in range(ITERS):
        if it > 0:
            rows = split_rows(v)
            for part in chunked(S):
                total = lax.dot_general(rows, gibbs[part, :], NT, preferred_element_type=jnp.float32)
                rbuf[it, me_c, :, part] = jnp.sum(total, axis=0, keepdims=True)
        out, u = exchange_rows(it)
        pending += out
        rows = split_rows(u)
        for part in chunked(T):
            total = lax.dot_general(rows, gibbs[:, part], NN, preferred_element_type=jnp.float32)
            cbuf[it, me_r, :, part] = jnp.sum(total, axis=0, keepdims=True)
        out, v = exchange_cols(it)
        pending += out

    last = ITERS - 1
    own = pl.ds(pl.multiple_of(me_c * m, m), m)
    total = rbuf[last, 0, :, own]
    for j in range(1, n_c):
        total = total + rbuf[last, j, :, own]
    spot_ref[...] = strength * jnp.log(smass_ref[...] / total)
    own = pl.ds(pl.multiple_of(me_r * m, m), m)
    total = cbuf[last, 0, :, own]
    for j in range(1, n_r):
        total = total + cbuf[last, j, :, own]
    tpot_ref[...] = strength * jnp.log(tmass_ref[...] / total)
    for copy in pending:
        copy.wait_send()


def per_device(source_emb, target_emb, source_mass, target_mass, cand_cols, cand_count):
    n_r, n_c = lax.axis_size("rows"), lax.axis_size("cols")
    m, w = source_emb.shape
    S, T = n_c * m, n_r * m
    vmem = pl.BlockSpec(memory_space=pltpu.VMEM)
    dma = pltpu.SemaphoreType.DMA
    spot, tpot = pl.pallas_call(
        functools.partial(kernel, n_r, n_c),
        out_shape=[jax.ShapeDtypeStruct((1, m), jnp.float32)] * 2,
        in_specs=[vmem] * 6,
        out_specs=[vmem] * 2,
        scratch_shapes=[
            pltpu.VMEM((n_c, m, w), jnp.bfloat16),
            pltpu.VMEM((n_r, m, w), jnp.bfloat16),
            pltpu.VMEM((n_c, 1, m), jnp.float32),
            pltpu.VMEM((n_r, 1, m), jnp.float32),
            pltpu.VMEM((cand_cols.shape[0], T), jnp.float32),
            pltpu.VMEM((S, T), jnp.bfloat16),
            pltpu.VMEM((ITERS, n_c, 1, S), jnp.float32),
            pltpu.VMEM((ITERS, n_r, 1, T), jnp.float32),
            dma((n_c - 1,)), dma((n_c - 1,)), dma((n_r - 1,)), dma((n_r - 1,)),
            dma((n_c - 1,)), dma((n_c - 1,)), dma((n_r - 1,)), dma((n_r - 1,)),
            dma((ITERS, n_c - 1)), dma((ITERS, n_c - 1)),
            dma((ITERS, n_r - 1)), dma((ITERS, n_r - 1)),
        ],
        compiler_params=pltpu.CompilerParams(
            collective_id=0, has_side_effects=True,
            vmem_limit_bytes=min(58 << 20, 2 * S * T + (24 << 20)),
        ),
        name="sinkhorn",
    )(source_emb, target_emb, source_mass.reshape(1, m), target_mass.reshape(1, m),
      cand_cols, cand_count)
    return spot.reshape(-1), tpot.reshape(-1)


def solution(mesh):
    placed = (
        P(("groups", "rows", "cols"), None),
        P(("groups", "cols", "rows"), None),
        P(("groups", "rows", "cols")),
        P(("groups", "cols", "rows")),
        P(("groups", "rows"), "cols"),
        P(("groups", "rows"), "cols"),
    )
    return jax.shard_map(
        per_device,
        mesh=mesh,
        in_specs=placed,
        out_specs=(P(("groups", "rows", "cols")), P(("groups", "cols", "rows"))),
        check_vma=False,
    )
```

```python
import functools
import math

import jax
import jax.numpy as jnp
from jax import lax
from jax.experimental import pallas as pl
from jax.experimental.pallas import tpu as pltpu
from jax.sharding import PartitionSpec as P

BS = 128
ITERS = 2
strength = 0.05
MESH = pl.DeviceIdType.MESH
NT = (((1,), (1,)), ((), ()))
NN = (((1,), (0,)), ((), ()))


def normalize(embed):
    values = embed.astype(jnp.float32)
    factor = lax.rsqrt(jnp.sum(values * values, axis=-1, keepdims=True) + 1e-06)
    return (values * factor).astype(jnp.bfloat16)


def split_rows(vector):
    high = vector.astype(jnp.bfloat16).astype(jnp.float32)
    row = lax.broadcasted_iota(jnp.int32, (16, vector.shape[1]), 0)
    rows = jnp.where(row == 0, high, jnp.where(row == 1, vector - high, 0.0))
    return rows.astype(jnp.bfloat16)


def kernel(
    n_r, n_c,
    src_hbm, tgt_hbm, smass_hbm, tmass_hbm, cand_hbm, count_hbm,
    pot_ref,
    src_ref, tgt_ref, cand_ref, count_ref, in_sem, sp, tp, sm, tm, mask, gibbs, rbuf, cbuf,
    s_send, s_recv, t_send, t_recv, sm_send, sm_recv, tm_send, tm_recv,
    r_send, r_recv, c_send, c_recv,
):
    me_r, me_c = lax.axis_index("rows"), lax.axis_index("cols")
    m = src_ref.shape[0]
    mb = m // BS
    S, T = n_c * m, n_r * m
    slots, blocks = cand_ref.shape
    relayed = n_c == 4

    def to_col(k):
        return lax.rem(me_c + k, n_c)

    def to_row(k):
        return lax.rem(me_r + k, n_r)

    sm_own, tm_own = sm.at[me_c], tm.at[me_r]
    loads = [
        pltpu.make_async_copy(a, b, in_sem.at[i]) for i, (a, b) in enumerate((
            (src_hbm, src_ref), (tgt_hbm, tgt_ref), (smass_hbm, sm_own),
            (tmass_hbm, tm_own), (cand_hbm, cand_ref), (count_hbm, count_ref)))
    ]
    for load in loads:
        load.start()

    barrier = pltpu.get_barrier_semaphore()
    for k in range(1, n_c):
        pl.semaphore_signal(barrier, inc=1, device_id={"cols": to_col(k)}, device_id_type=MESH)
    for k in range(1, n_r):
        pl.semaphore_signal(barrier, inc=1, device_id={"rows": to_row(k)}, device_id_type=MESH)

    loads[0].wait()
    sp[me_c] = normalize(src_ref[...])
    loads[1].wait()
    tp[me_r] = normalize(tgt_ref[...])
    for load in loads[2:]:
        load.wait()
    pl.semaphore_wait(barrier, n_c + n_r - 2)

    def col_copy(ref, send, recv, k):
        return pltpu.make_async_remote_copy(
            ref, ref, send, recv, device_id={"cols": to_col(k)}, device_id_type=MESH)

    def row_copy(ref, send, recv, k):
        return pltpu.make_async_remote_copy(
            ref, ref, send, recv, device_id={"rows": to_row(k)}, device_id_type=MESH)

    def piece(owner, h):
        return sp.at[owner, pl.ds(h * BS, BS)]

    def s_copy(owner, target, k, h):
        return pltpu.make_async_remote_copy(
            piece(owner, h), piece(owner, h), s_send.at[k - 1, h], s_recv.at[k - 1, h],
            device_id={"cols": target}, device_id_type=MESH)

    def s_arrive(owner, h):
        s_copy(owner, to_col(1), lax.rem(me_c + n_c - owner, n_c), h).wait_recv()

    inner = (me_c == 1) | (me_c == 2)
    if relayed:
        near = jnp.where(me_c >= 2, 3, 1)
        for k in (near, 4 - near):
            for h in range(mb):
                s_copy(me_c, to_col(k), k, h).start()

        @pl.when(jnp.logical_not(inner))
        def _():
            for h in range(mb):
                s_copy(me_c, to_col(2), 2, h).start()
    else:
        for k in range(1, n_c):
            for h in range(mb):
                s_copy(me_c, to_col(k), k, h).start()

    t_out = [row_copy(tp.at[me_r], t_send.at[k - 1], t_recv.at[k - 1], k) for k in range(1, n_r)]
    sm_out = [col_copy(sm.at[me_c], sm_send.at[k - 1], sm_recv.at[k - 1], k) for k in range(1, n_c)]
    tm_out = [row_copy(tm.at[me_r], tm_send.at[k - 1], tm_recv.at[k - 1], k) for k in range(1, n_r)]
    for copy in t_out + sm_out + tm_out:
        copy.start()

    def from_col(ref_of, send, recv, k):
        owner = lax.rem(me_c + n_c - k, n_c)
        col_copy(ref_of(owner), send, recv, k).wait_recv()

    def from_row(ref_of, send, recv, k):
        owner = lax.rem(me_r + n_r - k, n_r)
        row_copy(ref_of(owner), send, recv, k).wait_recv()

    target_block = lax.broadcasted_iota(jnp.int32, mask.shape, 1) // BS
    hit = jnp.zeros(mask.shape, jnp.float32)
    diagonal = (lax.broadcasted_iota(jnp.int32, (blocks, blocks), 0)
                == lax.broadcasted_iota(jnp.int32, (blocks, blocks), 1))

    def as_column(row):
        return jnp.sum(jnp.where(diagonal, row.astype(jnp.float32), 0.0), axis=1, keepdims=True)

    counts = as_column(count_ref[...])
    for k in range(slots):
        named = as_column(cand_ref[k:k + 1, :]).astype(jnp.int32)
        live = (named == target_block) & (counts > k)
        hit = jnp.where(live, 1.0, hit)
    mask[...] = hit

    first = 1 + lax.rem(me_c, 2)
    if relayed:
        for h in range(mb):
            s_arrive(first, h)

            @pl.when(inner)
            def _():
                s_copy(first, 3 * me_c - 3, 2, h).start()

    for k in range(1, n_r):
        from_row(lambda o: tp.at[o], t_send.at[k - 1], t_recv.at[k - 1], k)

    ones = jnp.ones((16, T), jnp.bfloat16)
    width = min(T, 1024)
    scale = math.log2(math.e) / strength

    def build(owner, awaited=True):
        for b in range(mb):
            if awaited:
                s_arrive(owner, b)
            block = sp[owner, b * BS:(b + 1) * BS, :]
            row0 = pl.multiple_of(owner * m + b * BS, BS)
            for t0 in range(0, n_r):
                sim = lax.dot_general(block, tp[t0], NT, preferred_element_type=jnp.float32)
                live = mask[pl.ds(owner * mb + b, 1), t0 * m:(t0 + 1) * m]
                gibbs[pl.ds(row0, BS), t0 * m:(t0 + 1) * m] = (
                    jnp.exp2(sim * scale) * live).astype(jnp.bfloat16)
        rows = pl.ds(pl.multiple_of(owner * m, m), m)
        total = lax.dot_general(ones, gibbs[rows, :], NT, preferred_element_type=jnp.float32)
        rbuf[0, me_c, :, rows] = total[:1]

    build(me_c, awaited=False)
    if relayed:
        build(first, awaited=False)
        build(3 * lax.rem(me_c + 1, 2))
        build(to_col(2))
    else:
        def arrive(k, carry):
            build(to_col(k))
            return carry

        lax.fori_loop(1, n_c, arrive, 0)

    def chunked(extent):
        step = min(extent, 1024)
        return [slice(i, i + step) for i in range(0, extent, step)]

    def exchange_rows(it):
        out = [col_copy(rbuf.at[it, me_c], r_send.at[it, k - 1], r_recv.at[it, k - 1], k)
               for k in range(1, n_c)]
        for copy in out:
            copy.start()
        if it == 0:
            for k in range(1, n_c):
                from_col(lambda o: sm.at[o], sm_send.at[k - 1], sm_recv.at[k - 1], k)
        for k in range(1, n_c):
            from_col(lambda o: rbuf.at[it, o], r_send.at[it, k - 1], r_recv.at[it, k - 1], k)
        total = rbuf[it, 0]
        for j in range(1, n_c):
            total = total + rbuf[it, j]
        return out, jnp.concatenate([sm[j] for j in range(n_c)], axis=1) / total

    def exchange_cols(it):
        out = [row_copy(cbuf.at[it, me_r], c_send.at[it, k - 1], c_recv.at[it, k - 1], k)
               for k in range(1, n_r)]
        for copy in out:
            copy.start()
        if it == 0:
            for k in range(1, n_r):
                from_row(lambda o: tm.at[o], tm_send.at[k - 1], tm_recv.at[k - 1], k)
        for k in range(1, n_r):
            from_row(lambda o: cbuf.at[it, o], c_send.at[it, k - 1], c_recv.at[it, k - 1], k)
        total = cbuf[it, 0]
        for j in range(1, n_r):
            total = total + cbuf[it, j]
        return out, jnp.concatenate([tm[j] for j in range(n_r)], axis=1) / total

    pending = t_out + sm_out + tm_out
    for it in range(ITERS):
        if it > 0:
            rows = split_rows(v)
            for part in chunked(S):
                total = lax.dot_general(rows, gibbs[part, :], NT, preferred_element_type=jnp.float32)
                rbuf[it, me_c, :, part] = jnp.sum(total, axis=0, keepdims=True)
        out, u = exchange_rows(it)
        pending += out
        rows = split_rows(u)
        for part in chunked(T):
            total = lax.dot_general(rows, gibbs[:, part], NN, preferred_element_type=jnp.float32)
            cbuf[it, me_r, :, part] = jnp.sum(total, axis=0, keepdims=True)
        out, v = exchange_cols(it)
        pending += out

    last = ITERS - 1
    own = pl.ds(pl.multiple_of(me_c * m, m), m)
    total = rbuf[last, 0, :, own]
    for j in range(1, n_c):
        total = total + rbuf[last, j, :, own]
    pot_ref[0:1] = strength * jnp.log(sm[me_c] / total)
    own = pl.ds(pl.multiple_of(me_r * m, m), m)
    total = cbuf[last, 0, :, own]
    for j in range(1, n_r):
        total = total + cbuf[last, j, :, own]
    pot_ref[1:2] = strength * jnp.log(tm[me_r] / total)
    for copy in pending:
        copy.wait_send()
    for k in range(1, n_c):
        for h in range(mb):
            s_copy(me_c, to_col(k), k, h).wait_send()


def per_device(source_emb, target_emb, source_mass, target_mass, cand_cols, cand_count):
    n_r, n_c = lax.axis_size("rows"), lax.axis_size("cols")
    m, w = source_emb.shape
    S, T = n_c * m, n_r * m
    vmem = pl.BlockSpec(memory_space=pltpu.VMEM)
    dma = pltpu.SemaphoreType.DMA
    slots, blocks = cand_cols.shape[1], cand_cols.shape[0]
    pots = pl.pallas_call(
        functools.partial(kernel, n_r, n_c),
        out_shape=jax.ShapeDtypeStruct((2, m), jnp.float32),
        in_specs=[pl.BlockSpec(memory_space=pltpu.HBM)] * 6,
        out_specs=vmem,
        scratch_shapes=[
            pltpu.VMEM((m, w), jnp.bfloat16),
            pltpu.VMEM((m, w), jnp.bfloat16),
            pltpu.VMEM((slots, blocks), jnp.int32),
            pltpu.VMEM((1, blocks), jnp.int32),
            dma((6,)),
            pltpu.VMEM((n_c, m, w), jnp.bfloat16),
            pltpu.VMEM((n_r, m, w), jnp.bfloat16),
            pltpu.VMEM((n_c, 1, m), jnp.float32),
            pltpu.VMEM((n_r, 1, m), jnp.float32),
            pltpu.VMEM((blocks, T), jnp.float32),
            pltpu.VMEM((S, T), jnp.bfloat16),
            pltpu.VMEM((ITERS, n_c, 1, S), jnp.float32),
            pltpu.VMEM((ITERS, n_r, 1, T), jnp.float32),
            dma((n_c - 1, m // BS)), dma((n_c - 1, m // BS)),
            dma((n_r - 1,)), dma((n_r - 1,)),
            dma((n_c - 1,)), dma((n_c - 1,)), dma((n_r - 1,)), dma((n_r - 1,)),
            dma((ITERS, n_c - 1)), dma((ITERS, n_c - 1)),
            dma((ITERS, n_r - 1)), dma((ITERS, n_r - 1)),
        ],
        compiler_params=pltpu.CompilerParams(
            collective_id=0, has_side_effects=True,
            vmem_limit_bytes=63 << 20,
        ),
        name="sinkhorn",
    )(source_emb, target_emb, source_mass.reshape(1, m), target_mass.reshape(1, m),
      cand_cols.T, cand_count.T)
    return pots[0], pots[1]


def solution(mesh):
    placed = (
        P(("groups", "rows", "cols"), None),
        P(("groups", "cols", "rows"), None),
        P(("groups", "rows", "cols")),
        P(("groups", "cols", "rows")),
        P(("groups", "rows"), "cols"),
        P(("groups", "rows"), "cols"),
    )
    return jax.shard_map(
        per_device,
        mesh=mesh,
        in_specs=placed,
        out_specs=(P(("groups", "rows", "cols")), P(("groups", "cols", "rows"))),
        check_vma=False,
    )
```

```python
import functools
import math

import jax
import jax.numpy as jnp
from jax import lax
from jax.experimental import pallas as pl
from jax.experimental.pallas import tpu as pltpu
from jax.sharding import PartitionSpec as P

BS = 128
ITERS = 2
strength = 0.05
MESH = pl.DeviceIdType.MESH
NT = (((1,), (1,)), ((), ()))
NN = (((1,), (0,)), ((), ()))


def normalize(embed):
    values = embed.astype(jnp.float32)
    factor = lax.rsqrt(jnp.sum(values * values, axis=-1, keepdims=True) + 1e-06)
    return (values * factor).astype(jnp.bfloat16)


def split_rows(vector):
    high = vector.astype(jnp.bfloat16).astype(jnp.float32)
    row = lax.broadcasted_iota(jnp.int32, (16, vector.shape[1]), 0)
    rows = jnp.where(row == 0, high, jnp.where(row == 1, vector - high, 0.0))
    return rows.astype(jnp.bfloat16)


def kernel(
    n_r, n_c,
    src_hbm, tgt_hbm, smass_hbm, tmass_hbm, cand_hbm, count_hbm,
    pot_ref,
    src_ref, tgt_ref, smine, cand_own, count_own, cand_ref, count_ref, pout, pin, in_sem, swap_send, swap_recv, sp, tp, sm, tm, mask, gibbs, rbuf, cbuf,
    s_send, s_recv, t_send, t_recv, sm_send, sm_recv, tm_send, tm_recv,
    r_send, r_recv, c_send, c_recv,
):
    me_r, me_c = lax.axis_index("rows"), lax.axis_index("cols")
    m = src_ref.shape[0]
    mb = m // BS
    S, T = n_c * m, n_r * m
    slots, blocks = cand_ref.shape
    relayed = n_c == 4
    odd = lax.rem(me_c, 2)

    def flip(row, bit):
        return row + bit * (1 - 2 * lax.rem(row, 2))

    role = flip(me_r, odd)

    def holder(row, col):
        return {"rows": flip(row, lax.rem(col, 2)), "cols": col}


    def to_col(k):
        return lax.rem(me_c + k, n_c)

    def to_row(k):
        return lax.rem(me_r + k, n_r)

    tm_own = tm.at[me_r]
    loads = [
        pltpu.make_async_copy(a, b, in_sem.at[i]) for i, (a, b) in enumerate((
            (src_hbm, src_ref), (tgt_hbm, tgt_ref), (smass_hbm, smine),
            (tmass_hbm, tm_own), (cand_hbm, cand_own), (count_hbm, count_own)))
    ]
    for load in loads:
        load.start()

    barrier = pltpu.get_barrier_semaphore()
    for k in range(1, n_c):
        for row in (me_r, flip(me_r, 1)):
            pl.semaphore_signal(
                barrier, inc=1, device_id={"rows": row, "cols": to_col(k)}, device_id_type=MESH)
    for k in range(1, n_r):
        pl.semaphore_signal(barrier, inc=1, device_id={"rows": to_row(k)}, device_id_type=MESH)

    loads[0].wait()
    src_ref[...] = normalize(src_ref[...])
    loads[1].wait()
    tp[me_r] = normalize(tgt_ref[...])
    for load in loads[2:]:
        load.wait()
    pl.semaphore_wait(barrier, 2 * (n_c - 1) + n_r - 1)

    def col_copy(src, dst, send, recv, k, row):
        return pltpu.make_async_remote_copy(
            src, dst, send, recv, device_id=holder(row, to_col(k)), device_id_type=MESH)

    def swap(i, src, dst):
        return pltpu.make_async_remote_copy(
            src, dst, swap_send.at[i], swap_recv.at[i],
            device_id={"rows": flip(me_r, 1)}, device_id_type=MESH)

    swaps = [
        swap(0, src_ref, sp.at[me_c]), swap(1, smine, sm.at[me_c]),
        swap(2, cand_own, cand_ref), swap(3, count_own, count_ref),
    ]

    def row_copy(ref, send, recv, k):
        return pltpu.make_async_remote_copy(
            ref, ref, send, recv, device_id={"rows": to_row(k)}, device_id_type=MESH)

    def piece(owner, h):
        return sp.at[owner, pl.ds(h * BS, BS)]

    def s_copy(owner, target, k, h, src=None):
        row = me_r if src is not None else role
        return pltpu.make_async_remote_copy(
            piece(owner, h) if src is None else src, piece(owner, h),
            s_send.at[k - 1, h], s_recv.at[k - 1, h],
            device_id=holder(row, target), device_id_type=MESH)

    def own_copy(k, h):
        return s_copy(me_c, to_col(k), k, h, src_ref.at[pl.ds(h * BS, BS)])

    def s_arrive(owner, h):
        s_copy(owner, to_col(1), lax.rem(me_c + n_c - owner, n_c), h).wait_recv()

    inner = (me_c == 1) | (me_c == 2)
    if relayed:
        near = jnp.where(me_c >= 2, 3, 1)
        for k in (near, 4 - near):
            for h in range(mb):
                own_copy(k, h).start()

        @pl.when(jnp.logical_not(inner))
        def _():
            for h in range(mb):
                own_copy(2, h).start()
    else:
        for k in range(1, n_c):
            for h in range(mb):
                own_copy(k, h).start()

    @pl.when(odd == 1)
    def _():
        for copy in swaps:
            copy.start()

    @pl.when(odd == 0)
    def _():
        sp[me_c] = src_ref[...]
        sm[me_c] = smine[...]
        cand_ref[...] = cand_own[...]
        count_ref[...] = count_own[...]

    t_out = [row_copy(tp.at[me_r], t_send.at[k - 1], t_recv.at[k - 1], k) for k in range(1, n_r)]
    sm_out = [col_copy(smine, sm.at[me_c], sm_send.at[k - 1], sm_recv.at[k - 1], k, me_r)
              for k in range(1, n_c)]
    tm_out = [row_copy(tm.at[me_r], tm_send.at[k - 1], tm_recv.at[k - 1], k) for k in range(1, n_r)]
    for copy in t_out + sm_out + tm_out:
        copy.start()

    def from_col(ref_of, send, recv, k):
        owner = lax.rem(me_c + n_c - k, n_c)
        col_copy(ref_of(owner), ref_of(owner), send, recv, k, role).wait_recv()

    def from_row(ref_of, send, recv, k):
        owner = lax.rem(me_r + n_r - k, n_r)
        row_copy(ref_of(owner), send, recv, k).wait_recv()

    @pl.when(odd == 1)
    def _():
        for copy in swaps:
            copy.wait_recv()

    target_block = lax.broadcasted_iota(jnp.int32, mask.shape, 1) // BS
    hit = jnp.zeros(mask.shape, jnp.float32)
    diagonal = (lax.broadcasted_iota(jnp.int32, (blocks, blocks), 0)
                == lax.broadcasted_iota(jnp.int32, (blocks, blocks), 1))

    def as_column(row):
        return jnp.sum(jnp.where(diagonal, row.astype(jnp.float32), 0.0), axis=1, keepdims=True)

    counts = as_column(count_ref[...])
    for k in range(slots):
        named = as_column(cand_ref[k:k + 1, :]).astype(jnp.int32)
        live = (named == target_block) & (counts > k)
        hit = jnp.where(live, 1.0, hit)
    mask[...] = hit

    first = 1 + lax.rem(me_c, 2)
    if relayed:
        for h in range(mb):
            s_arrive(first, h)

            @pl.when(inner)
            def _():
                s_copy(first, 3 * me_c - 3, 2, h).start()

    for k in range(1, n_r):
        from_row(lambda o: tp.at[o], t_send.at[k - 1], t_recv.at[k - 1], k)

    ones = jnp.ones((16, T), jnp.bfloat16)
    width = min(T, 1024)
    scale = math.log2(math.e) / strength

    def build(owner, awaited=True):
        for b in range(mb):
            if awaited:
                s_arrive(owner, b)
            block = sp[owner, b * BS:(b + 1) * BS, :]
            row0 = pl.multiple_of(owner * m + b * BS, BS)
            for t0 in range(0, n_r):
                sim = lax.dot_general(block, tp[t0], NT, preferred_element_type=jnp.float32)
                live = mask[pl.ds(owner * mb + b, 1), t0 * m:(t0 + 1) * m]
                gibbs[pl.ds(row0, BS), t0 * m:(t0 + 1) * m] = (
                    jnp.exp2(sim * scale) * live).astype(jnp.bfloat16)
        rows = pl.ds(pl.multiple_of(owner * m, m), m)
        total = lax.dot_general(ones, gibbs[rows, :], NT, preferred_element_type=jnp.float32)
        rbuf[0, me_c, :, rows] = total[:1]

    build(me_c, awaited=False)
    if relayed:
        build(first, awaited=False)
        build(3 * lax.rem(me_c + 1, 2))
        build(to_col(2))
    else:
        def arrive(k, carry):
            build(to_col(k))
            return carry

        lax.fori_loop(1, n_c, arrive, 0)

    def chunked(extent):
        step = min(extent, 1024)
        return [slice(i, i + step) for i in range(0, extent, step)]

    def exchange_rows(it):
        out = [col_copy(rbuf.at[it, me_c], rbuf.at[it, me_c],
                        r_send.at[it, k - 1], r_recv.at[it, k - 1], k, role)
               for k in range(1, n_c)]
        for copy in out:
            copy.start()
        if it == 0:
            for k in range(1, n_c):
                from_col(lambda o: sm.at[o], sm_send.at[k - 1], sm_recv.at[k - 1], k)
        for k in range(1, n_c):
            from_col(lambda o: rbuf.at[it, o], r_send.at[it, k - 1], r_recv.at[it, k - 1], k)
        total = rbuf[it, 0]
        for j in range(1, n_c):
            total = total + rbuf[it, j]
        return out, jnp.concatenate([sm[j] for j in range(n_c)], axis=1) / total

    pending = t_out + sm_out + tm_out
    home = swap(4, pout, pin)

    def source_side():
        own = pl.ds(pl.multiple_of(me_c * m, m), m)
        total = rbuf[ITERS - 1, 0, :, own]
        for j in range(1, n_c):
            total = total + rbuf[ITERS - 1, j, :, own]
        pout[...] = strength * jnp.log(sm[me_c] / total)

        @pl.when(odd == 1)
        def _():
            home.start()
            for copy in swaps:
                copy.wait_send()

        for copy in pending:
            copy.wait_send()
        for k in range(1, n_c):
            for h in range(mb):
                own_copy(k, h).wait_send()

        @pl.when(odd == 1)
        def _():
            home.wait()
            pot_ref[0:1] = pin[...]

        @pl.when(odd == 0)
        def _():
            pot_ref[0:1] = pout[...]

    def exchange_cols(it):
        out = [row_copy(cbuf.at[it, me_r], c_send.at[it, k - 1], c_recv.at[it, k - 1], k)
               for k in range(1, n_r)]
        for copy in out:
            copy.start()
        if it == ITERS - 1:
            source_side()
        if it == 0:
            for k in range(1, n_r):
                from_row(lambda o: tm.at[o], tm_send.at[k - 1], tm_recv.at[k - 1], k)
        for k in range(1, n_r):
            from_row(lambda o: cbuf.at[it, o], c_send.at[it, k - 1], c_recv.at[it, k - 1], k)
        total = cbuf[it, 0]
        for j in range(1, n_r):
            total = total + cbuf[it, j]
        return out, jnp.concatenate([tm[j] for j in range(n_r)], axis=1) / total

    for it in range(ITERS):
        if it > 0:
            rows = split_rows(v)
            for part in chunked(S):
                total = lax.dot_general(rows, gibbs[part, :], NT, preferred_element_type=jnp.float32)
                rbuf[it, me_c, :, part] = jnp.sum(total, axis=0, keepdims=True)
        out, u = exchange_rows(it)
        pending += out
        rows = split_rows(u)
        for part in chunked(T):
            total = lax.dot_general(rows, gibbs[:, part], NN, preferred_element_type=jnp.float32)
            cbuf[it, me_r, :, part] = jnp.sum(total, axis=0, keepdims=True)
        out, v = exchange_cols(it)
        if it < ITERS - 1:
            pending += out

    last = ITERS - 1
    own = pl.ds(pl.multiple_of(me_r * m, m), m)
    total = cbuf[last, 0, :, own]
    for j in range(1, n_r):
        total = total + cbuf[last, j, :, own]
    pot_ref[1:2] = strength * jnp.log(tm[me_r] / total)
    for copy in out:
        copy.wait_send()


def per_device(source_emb, target_emb, source_mass, target_mass, cand_cols, cand_count):
    n_r, n_c = lax.axis_size("rows"), lax.axis_size("cols")
    m, w = source_emb.shape
    S, T = n_c * m, n_r * m
    vmem = pl.BlockSpec(memory_space=pltpu.VMEM)
    dma = pltpu.SemaphoreType.DMA
    slots, blocks = cand_cols.shape[1], cand_cols.shape[0]
    pots = pl.pallas_call(
        functools.partial(kernel, n_r, n_c),
        out_shape=jax.ShapeDtypeStruct((2, m), jnp.float32),
        in_specs=[pl.BlockSpec(memory_space=pltpu.HBM)] * 6,
        out_specs=vmem,
        scratch_shapes=[
            pltpu.VMEM((m, w), jnp.bfloat16),
            pltpu.VMEM((m, w), jnp.bfloat16),
            pltpu.VMEM((1, m), jnp.float32),
            pltpu.VMEM((slots, blocks), jnp.int32),
            pltpu.VMEM((1, blocks), jnp.int32),
            pltpu.VMEM((slots, blocks), jnp.int32),
            pltpu.VMEM((1, blocks), jnp.int32),
            pltpu.VMEM((1, m), jnp.float32),
            pltpu.VMEM((1, m), jnp.float32),
            dma((6,)), dma((5,)), dma((5,)),
            pltpu.VMEM((n_c, m, w), jnp.bfloat16),
            pltpu.VMEM((n_r, m, w), jnp.bfloat16),
            pltpu.VMEM((n_c, 1, m), jnp.float32),
            pltpu.VMEM((n_r, 1, m), jnp.float32),
            pltpu.VMEM((blocks, T), jnp.float32),
            pltpu.VMEM((S, T), jnp.bfloat16),
            pltpu.VMEM((ITERS, n_c, 1, S), jnp.float32),
            pltpu.VMEM((ITERS, n_r, 1, T), jnp.float32),
            dma((n_c - 1, m // BS)), dma((n_c - 1, m // BS)),
            dma((n_r - 1,)), dma((n_r - 1,)),
            dma((n_c - 1,)), dma((n_c - 1,)), dma((n_r - 1,)), dma((n_r - 1,)),
            dma((ITERS, n_c - 1)), dma((ITERS, n_c - 1)),
            dma((ITERS, n_r - 1)), dma((ITERS, n_r - 1)),
        ],
        compiler_params=pltpu.CompilerParams(
            collective_id=0, has_side_effects=True,
            vmem_limit_bytes=63 << 20,
        ),
        name="sinkhorn",
    )(source_emb, target_emb, source_mass.reshape(1, m), target_mass.reshape(1, m),
      cand_cols.T, cand_count.T)
    return pots[0], pots[1]


def solution(mesh):
    placed = (
        P(("groups", "rows", "cols"), None),
        P(("groups", "cols", "rows"), None),
        P(("groups", "rows", "cols")),
        P(("groups", "cols", "rows")),
        P(("groups", "rows"), "cols"),
        P(("groups", "rows"), "cols"),
    )
    return jax.shard_map(
        per_device,
        mesh=mesh,
        in_specs=placed,
        out_specs=(P(("groups", "rows", "cols")), P(("groups", "cols", "rows"))),
        check_vma=False,
    )
```

```python
import functools
import math

import jax
import jax.numpy as jnp
from jax import lax
from jax.experimental import pallas as pl
from jax.experimental.pallas import tpu as pltpu
from jax.sharding import PartitionSpec as P

BS = 128
ITERS = 2
strength = 0.05
MESH = pl.DeviceIdType.MESH
NT = (((1,), (1,)), ((), ()))
NN = (((1,), (0,)), ((), ()))


def normalize(embed):
    values = embed.astype(jnp.float32)
    factor = lax.rsqrt(jnp.sum(values * values, axis=-1, keepdims=True) + 1e-06)
    return (values * factor).astype(jnp.bfloat16)


def split_rows(vector):
    high = vector.astype(jnp.bfloat16).astype(jnp.float32)
    row = lax.broadcasted_iota(jnp.int32, (16, vector.shape[1]), 0)
    rows = jnp.where(row == 0, high, jnp.where(row == 1, vector - high, 0.0))
    return rows.astype(jnp.bfloat16)


def kernel(
    n_r, n_c,
    src_hbm, tgt_hbm, smass_hbm, tmass_hbm, cand_hbm, count_hbm,
    pot_ref,
    src_ref, tgt_ref, smine, cand_own, count_own, cand_ref, count_ref, pout, pin, in_sem, swap_send, swap_recv, sp, tp, sm, tm, mask, gibbs, rbuf, cbuf,
    s_send, s_recv, t_send, t_recv, sm_send, sm_recv, tm_send, tm_recv,
    r_send, r_recv, c_send, c_recv,
):
    me_r, me_c = lax.axis_index("rows"), lax.axis_index("cols")
    m = src_ref.shape[0]
    mb = m // BS
    S, T = n_c * m, n_r * m
    slots, blocks = cand_ref.shape
    relayed = n_c == 4
    odd = lax.rem(me_c, 2)

    def flip(row, bit):
        return row + bit * (1 - 2 * lax.rem(row, 2))

    role = flip(me_r, odd)

    def holder(row, col):
        return {"rows": flip(row, lax.rem(col, 2)), "cols": col}


    def to_col(k):
        return lax.rem(me_c + k, n_c)

    def to_row(k):
        return lax.rem(me_r + k, n_r)

    tm_own = tm.at[me_r]
    loads = [
        pltpu.make_async_copy(a, b, in_sem.at[i]) for i, (a, b) in enumerate((
            (src_hbm, src_ref), (tgt_hbm, tgt_ref), (smass_hbm, smine),
            (tmass_hbm, tm_own), (cand_hbm, cand_own), (count_hbm, count_own)))
    ]
    for load in loads:
        load.start()

    barrier = pltpu.get_barrier_semaphore()
    for k in range(1, n_c):
        for row in (me_r, flip(me_r, 1)):
            pl.semaphore_signal(
                barrier, inc=1, device_id={"rows": row, "cols": to_col(k)}, device_id_type=MESH)
    for k in range(1, n_r):
        pl.semaphore_signal(barrier, inc=1, device_id={"rows": to_row(k)}, device_id_type=MESH)

    loads[0].wait()
    src_ref[...] = normalize(src_ref[...])
    loads[1].wait()
    tp[me_r] = normalize(tgt_ref[...])
    for load in loads[2:]:
        load.wait()
    pl.semaphore_wait(barrier, 2 * (n_c - 1) + n_r - 1)

    def col_copy(src, dst, send, recv, k, row):
        return pltpu.make_async_remote_copy(
            src, dst, send, recv, device_id=holder(row, to_col(k)), device_id_type=MESH)

    def swap(i, src, dst):
        return pltpu.make_async_remote_copy(
            src, dst, swap_send.at[i], swap_recv.at[i],
            device_id={"rows": flip(me_r, 1)}, device_id_type=MESH)

    swaps = [
        swap(0, src_ref, sp.at[me_c]), swap(1, smine, sm.at[me_c]),
        swap(2, cand_own, cand_ref), swap(3, count_own, count_ref),
    ]

    def row_copy(ref, send, recv, k):
        return pltpu.make_async_remote_copy(
            ref, ref, send, recv, device_id={"rows": to_row(k)}, device_id_type=MESH)

    def piece(owner, h):
        return sp.at[owner, pl.ds(h * BS, BS)]

    def s_copy(owner, target, k, h, src=None):
        row = me_r if src is not None else role
        return pltpu.make_async_remote_copy(
            piece(owner, h) if src is None else src, piece(owner, h),
            s_send.at[k - 1, h], s_recv.at[k - 1, h],
            device_id=holder(row, target), device_id_type=MESH)

    def own_copy(k, h):
        return s_copy(me_c, to_col(k), k, h, src_ref.at[pl.ds(h * BS, BS)])

    def s_arrive(owner, h):
        s_copy(owner, to_col(1), lax.rem(me_c + n_c - owner, n_c), h).wait_recv()

    inner = (me_c == 1) | (me_c == 2)
    if relayed:
        near = jnp.where(me_c >= 2, 3, 1)
        for k in (near, 4 - near):
            for h in range(mb):
                own_copy(k, h).start()

        @pl.when(jnp.logical_not(inner))
        def _():
            for h in range(mb):
                own_copy(2, h).start()
    else:
        for k in range(1, n_c):
            for h in range(mb):
                own_copy(k, h).start()

    @pl.when(odd == 1)
    def _():
        for copy in swaps:
            copy.start()

    @pl.when(odd == 0)
    def _():
        sp[me_c] = src_ref[...]
        sm[me_c] = smine[...]
        cand_ref[...] = cand_own[...]
        count_ref[...] = count_own[...]

    t_out = [row_copy(tp.at[me_r], t_send.at[k - 1], t_recv.at[k - 1], k) for k in range(1, n_r)]
    sm_out = [col_copy(smine, sm.at[me_c], sm_send.at[k - 1], sm_recv.at[k - 1], k, me_r)
              for k in range(1, n_c)]
    tm_out = [row_copy(tm.at[me_r], tm_send.at[k - 1], tm_recv.at[k - 1], k) for k in range(1, n_r)]
    for copy in t_out + sm_out + tm_out:
        copy.start()

    def from_col(ref_of, send, recv, k):
        owner = lax.rem(me_c + n_c - k, n_c)
        col_copy(ref_of(owner), ref_of(owner), send, recv, k, role).wait_recv()

    def from_row(ref_of, send, recv, k):
        owner = lax.rem(me_r + n_r - k, n_r)
        row_copy(ref_of(owner), send, recv, k).wait_recv()

    first = 1 + lax.rem(me_c, 2)
    if relayed:
        for h in range(mb):
            s_arrive(first, h)

            @pl.when(inner)
            def _():
                s_copy(first, 3 * me_c - 3, 2, h).start()

    @pl.when(odd == 1)
    def _():
        for copy in swaps:
            copy.wait_recv()

    target_block = lax.broadcasted_iota(jnp.int32, mask.shape, 1) // BS
    hit = jnp.zeros(mask.shape, jnp.float32)
    diagonal = (lax.broadcasted_iota(jnp.int32, (blocks, blocks), 0)
                == lax.broadcasted_iota(jnp.int32, (blocks, blocks), 1))

    def as_column(row):
        return jnp.sum(jnp.where(diagonal, row.astype(jnp.float32), 0.0), axis=1, keepdims=True)

    counts = as_column(count_ref[...])
    for k in range(slots):
        named = as_column(cand_ref[k:k + 1, :]).astype(jnp.int32)
        live = (named == target_block) & (counts > k)
        hit = jnp.where(live, 1.0, hit)
    mask[...] = hit

    ones = jnp.ones((16, T), jnp.bfloat16)
    scale = math.log2(math.e) / strength

    def tile(owner, b, t):
        block = sp[owner, b * BS:(b + 1) * BS, :]
        row0 = pl.multiple_of(owner * m + b * BS, BS)
        columns = pl.ds(pl.multiple_of(t * m, m), m)
        sim = lax.dot_general(block, tp[t], NT, preferred_element_type=jnp.float32)
        live = mask[pl.ds(owner * mb + b, 1), columns]
        gibbs[pl.ds(row0, BS), columns] = (jnp.exp2(sim * scale) * live).astype(jnp.bfloat16)

    def row_total(owner, b):
        rows = pl.ds(pl.multiple_of(owner * m + b * BS, BS), BS)
        total = lax.dot_general(ones, gibbs[rows, :], NT, preferred_element_type=jnp.float32)
        rbuf[0, me_c, :, rows] = total[:1]

    def build(owner):
        for b in range(mb):
            s_arrive(owner, b)
            for t in range(n_r):
                tile(owner, b, t)
            row_total(owner, b)

    here = (me_c, first) if relayed else (me_c,)
    near_row = 3 - 2 * lax.rem(me_r, 2) if n_r == 4 else 1
    for k in (0, near_row, 4 - near_row, 2) if n_r == 4 else range(n_r):
        t = lax.rem(me_r + n_r - k, n_r)
        if not (isinstance(k, int) and k == 0):
            row_copy(tp.at[t], t_send.at[k - 1], t_recv.at[k - 1], k).wait_recv()
        for owner in here:
            for b in range(mb):
                tile(owner, b, t)
    for owner in here:
        for b in range(mb):
            row_total(owner, b)
    if relayed:
        build(3 * lax.rem(me_c + 1, 2))
        build(to_col(2))
    else:
        def arrive(k, carry):
            build(to_col(k))
            return carry

        lax.fori_loop(1, n_c, arrive, 0)

    def chunked(extent):
        step = min(extent, 1024)
        return [slice(i, i + step) for i in range(0, extent, step)]

    def exchange_rows(it):
        out = [col_copy(rbuf.at[it, me_c], rbuf.at[it, me_c],
                        r_send.at[it, k - 1], r_recv.at[it, k - 1], k, role)
               for k in range(1, n_c)]
        for copy in out:
            copy.start()
        if it == 0:
            for k in range(1, n_c):
                from_col(lambda o: sm.at[o], sm_send.at[k - 1], sm_recv.at[k - 1], k)
        for k in range(1, n_c):
            from_col(lambda o: rbuf.at[it, o], r_send.at[it, k - 1], r_recv.at[it, k - 1], k)
        total = rbuf[it, 0]
        for j in range(1, n_c):
            total = total + rbuf[it, j]
        return out, jnp.concatenate([sm[j] for j in range(n_c)], axis=1) / total

    pending = t_out + sm_out + tm_out
    home = swap(4, pout, pin)

    def source_side():
        own = pl.ds(pl.multiple_of(me_c * m, m), m)
        total = rbuf[ITERS - 1, 0, :, own]
        for j in range(1, n_c):
            total = total + rbuf[ITERS - 1, j, :, own]
        pout[...] = strength * jnp.log(sm[me_c] / total)

        @pl.when(odd == 1)
        def _():
            home.start()
            for copy in swaps:
                copy.wait_send()

        for copy in pending:
            copy.wait_send()
        for k in range(1, n_c):
            for h in range(mb):
                own_copy(k, h).wait_send()

        @pl.when(odd == 1)
        def _():
            home.wait()
            pot_ref[0:1] = pin[...]

        @pl.when(odd == 0)
        def _():
            pot_ref[0:1] = pout[...]

    def exchange_cols(it):
        out = [row_copy(cbuf.at[it, me_r], c_send.at[it, k - 1], c_recv.at[it, k - 1], k)
               for k in range(1, n_r)]
        for copy in out:
            copy.start()
        if it == ITERS - 1:
            source_side()
        if it == 0:
            for k in range(1, n_r):
                from_row(lambda o: tm.at[o], tm_send.at[k - 1], tm_recv.at[k - 1], k)
        for k in range(1, n_r):
            from_row(lambda o: cbuf.at[it, o], c_send.at[it, k - 1], c_recv.at[it, k - 1], k)
        total = cbuf[it, 0]
        for j in range(1, n_r):
            total = total + cbuf[it, j]
        return out, jnp.concatenate([tm[j] for j in range(n_r)], axis=1) / total

    for it in range(ITERS):
        if it > 0:
            rows = split_rows(v)
            for part in chunked(S):
                total = lax.dot_general(rows, gibbs[part, :], NT, preferred_element_type=jnp.float32)
                rbuf[it, me_c, :, part] = jnp.sum(total, axis=0, keepdims=True)
        out, u = exchange_rows(it)
        pending += out
        rows = split_rows(u)
        for part in chunked(T):
            total = lax.dot_general(rows, gibbs[:, part], NN, preferred_element_type=jnp.float32)
            cbuf[it, me_r, :, part] = jnp.sum(total, axis=0, keepdims=True)
        out, v = exchange_cols(it)
        if it < ITERS - 1:
            pending += out

    last = ITERS - 1
    own = pl.ds(pl.multiple_of(me_r * m, m), m)
    total = cbuf[last, 0, :, own]
    for j in range(1, n_r):
        total = total + cbuf[last, j, :, own]
    pot_ref[1:2] = strength * jnp.log(tm[me_r] / total)
    for copy in out:
        copy.wait_send()


def per_device(source_emb, target_emb, source_mass, target_mass, cand_cols, cand_count):
    n_r, n_c = lax.axis_size("rows"), lax.axis_size("cols")
    m, w = source_emb.shape
    S, T = n_c * m, n_r * m
    vmem = pl.BlockSpec(memory_space=pltpu.VMEM)
    dma = pltpu.SemaphoreType.DMA
    slots, blocks = cand_cols.shape[1], cand_cols.shape[0]
    pots = pl.pallas_call(
        functools.partial(kernel, n_r, n_c),
        out_shape=jax.ShapeDtypeStruct((2, m), jnp.float32),
        in_specs=[pl.BlockSpec(memory_space=pltpu.HBM)] * 6,
        out_specs=vmem,
        scratch_shapes=[
            pltpu.VMEM((m, w), jnp.bfloat16),
            pltpu.VMEM((m, w), jnp.bfloat16),
            pltpu.VMEM((1, m), jnp.float32),
            pltpu.VMEM((slots, blocks), jnp.int32),
            pltpu.VMEM((1, blocks), jnp.int32),
            pltpu.VMEM((slots, blocks), jnp.int32),
            pltpu.VMEM((1, blocks), jnp.int32),
            pltpu.VMEM((1, m), jnp.float32),
            pltpu.VMEM((1, m), jnp.float32),
            dma((6,)), dma((5,)), dma((5,)),
            pltpu.VMEM((n_c, m, w), jnp.bfloat16),
            pltpu.VMEM((n_r, m, w), jnp.bfloat16),
            pltpu.VMEM((n_c, 1, m), jnp.float32),
            pltpu.VMEM((n_r, 1, m), jnp.float32),
            pltpu.VMEM((blocks, T), jnp.float32),
            pltpu.VMEM((S, T), jnp.bfloat16),
            pltpu.VMEM((ITERS, n_c, 1, S), jnp.float32),
            pltpu.VMEM((ITERS, n_r, 1, T), jnp.float32),
            dma((n_c - 1, m // BS)), dma((n_c - 1, m // BS)),
            dma((n_r - 1,)), dma((n_r - 1,)),
            dma((n_c - 1,)), dma((n_c - 1,)), dma((n_r - 1,)), dma((n_r - 1,)),
            dma((ITERS, n_c - 1)), dma((ITERS, n_c - 1)),
            dma((ITERS, n_r - 1)), dma((ITERS, n_r - 1)),
        ],
        compiler_params=pltpu.CompilerParams(
            collective_id=0, has_side_effects=True,
            vmem_limit_bytes=63 << 20,
        ),
        name="sinkhorn",
    )(source_emb, target_emb, source_mass.reshape(1, m), target_mass.reshape(1, m),
      cand_cols.T, cand_count.T)
    return pots[0], pots[1]


def solution(mesh):
    placed = (
        P(("groups", "rows", "cols"), None),
        P(("groups", "cols", "rows"), None),
        P(("groups", "rows", "cols")),
        P(("groups", "cols", "rows")),
        P(("groups", "rows"), "cols"),
        P(("groups", "rows"), "cols"),
    )
    return jax.shard_map(
        per_device,
        mesh=mesh,
        in_specs=placed,
        out_specs=(P(("groups", "rows", "cols")), P(("groups", "cols", "rows"))),
        check_vma=False,
    )
```

```python
import functools
import math

import jax
import jax.numpy as jnp
from jax import lax
from jax.experimental import pallas as pl
from jax.experimental.pallas import tpu as pltpu
from jax.sharding import PartitionSpec as P

BS = 128
ITERS = 2
strength = 0.05
MESH = pl.DeviceIdType.MESH
NT = (((1,), (1,)), ((), ()))
NN = (((1,), (0,)), ((), ()))


def normalize(embed):
    values = embed.astype(jnp.float32)
    factor = lax.rsqrt(jnp.sum(values * values, axis=-1, keepdims=True) + 1e-06)
    return (values * factor).astype(jnp.bfloat16)


def split_rows(vector):
    high = vector.astype(jnp.bfloat16).astype(jnp.float32)
    row = lax.broadcasted_iota(jnp.int32, (16, vector.shape[1]), 0)
    rows = jnp.where(row == 0, high, jnp.where(row == 1, vector - high, 0.0))
    return rows.astype(jnp.bfloat16)


def kernel(
    n_r, n_c,
    src_hbm, tgt_hbm, smass_hbm, tmass_hbm, cand_hbm, count_hbm,
    pot_ref,
    src_ref, tgt_ref, smine, cand_own, count_own, cand_ref, count_ref, pout, pin, in_sem, swap_send, swap_recv, sp, tp, sm, tm, mask, gibbs, rbuf, cbuf,
    s_send, s_recv, t_send, t_recv, sm_send, sm_recv, tm_send, tm_recv,
    r_send, r_recv, c_send, c_recv,
):
    me_r, me_c = lax.axis_index("rows"), lax.axis_index("cols")
    m = src_ref.shape[0]
    mb = m // BS
    S, T = n_c * m, n_r * m
    slots, blocks = cand_ref.shape
    relayed = n_c == 4
    odd = lax.rem(me_c, 2)

    def flip(row, bit):
        return row + bit * (1 - 2 * lax.rem(row, 2))

    role = flip(me_r, odd)

    def holder(row, col):
        return {"rows": flip(row, lax.rem(col, 2)), "cols": col}


    def to_col(k):
        return lax.rem(me_c + k, n_c)

    def to_row(k):
        return lax.rem(me_r + k, n_r)

    tm_own = tm.at[me_r]
    loads = [
        pltpu.make_async_copy(a, b, in_sem.at[i]) for i, (a, b) in enumerate((
            (src_hbm, src_ref), (tgt_hbm, tgt_ref), (smass_hbm, smine),
            (tmass_hbm, tm_own), (cand_hbm, cand_own), (count_hbm, count_own)))
    ]
    for load in loads:
        load.start()

    barrier = pltpu.get_barrier_semaphore()
    for k in range(1, n_c):
        for row in (me_r, flip(me_r, 1)):
            pl.semaphore_signal(
                barrier, inc=1, device_id={"rows": row, "cols": to_col(k)}, device_id_type=MESH)
    for k in range(1, n_r):
        pl.semaphore_signal(barrier, inc=1, device_id={"rows": to_row(k)}, device_id_type=MESH)

    loads[0].wait()
    src_ref[...] = normalize(src_ref[...])
    loads[1].wait()
    tp[me_r] = normalize(tgt_ref[...])
    for load in loads[2:]:
        load.wait()
    pl.semaphore_wait(barrier, 2 * (n_c - 1) + n_r - 1)

    def col_copy(src, dst, send, recv, k, row):
        return pltpu.make_async_remote_copy(
            src, dst, send, recv, device_id=holder(row, to_col(k)), device_id_type=MESH)

    def swap(i, src, dst):
        return pltpu.make_async_remote_copy(
            src, dst, swap_send.at[i], swap_recv.at[i],
            device_id={"rows": flip(me_r, 1)}, device_id_type=MESH)

    swaps = [
        swap(0, src_ref, sp.at[me_c]), swap(1, smine, sm.at[me_c]),
        swap(2, cand_own, cand_ref), swap(3, count_own, count_ref),
    ]

    def row_copy(ref, send, recv, k):
        return pltpu.make_async_remote_copy(
            ref, ref, send, recv, device_id={"rows": to_row(k)}, device_id_type=MESH)

    def piece(owner, h):
        return sp.at[owner, pl.ds(h * BS, BS)]

    def s_copy(owner, target, k, h, src=None):
        row = me_r if src is not None else role
        return pltpu.make_async_remote_copy(
            piece(owner, h) if src is None else src, piece(owner, h),
            s_send.at[k - 1, h], s_recv.at[k - 1, h],
            device_id=holder(row, target), device_id_type=MESH)

    def own_copy(k, h):
        return s_copy(me_c, to_col(k), k, h, src_ref.at[pl.ds(h * BS, BS)])

    def s_arrive(owner, h):
        s_copy(owner, to_col(1), lax.rem(me_c + n_c - owner, n_c), h).wait_recv()

    inner = (me_c == 1) | (me_c == 2)
    if relayed:
        near = jnp.where(me_c >= 2, 3, 1)
        for k in (near, 4 - near):
            for h in range(mb):
                own_copy(k, h).start()

        @pl.when(jnp.logical_not(inner))
        def _():
            for h in range(mb):
                own_copy(2, h).start()
    else:
        for k in range(1, n_c):
            for h in range(mb):
                own_copy(k, h).start()

    @pl.when(odd == 1)
    def _():
        for copy in swaps:
            copy.start()

    @pl.when(odd == 0)
    def _():
        sp[me_c] = src_ref[...]
        sm[me_c] = smine[...]
        cand_ref[...] = cand_own[...]
        count_ref[...] = count_own[...]

    t_out = [row_copy(tp.at[me_r], t_send.at[k - 1], t_recv.at[k - 1], k) for k in range(1, n_r)]
    sm_out = [col_copy(smine, sm.at[me_c], sm_send.at[k - 1], sm_recv.at[k - 1], k, me_r)
              for k in range(1, n_c)]
    tm_out = [row_copy(tm.at[me_r], tm_send.at[k - 1], tm_recv.at[k - 1], k) for k in range(1, n_r)]
    for copy in t_out + sm_out + tm_out:
        copy.start()

    def from_col(ref_of, send, recv, k):
        owner = lax.rem(me_c + n_c - k, n_c)
        col_copy(ref_of(owner), ref_of(owner), send, recv, k, role).wait_recv()

    def from_row(ref_of, send, recv, k):
        owner = lax.rem(me_r + n_r - k, n_r)
        row_copy(ref_of(owner), send, recv, k).wait_recv()

    first = 1 + lax.rem(me_c, 2)
    if relayed:
        for h in range(mb):
            s_arrive(first, h)

            @pl.when(inner)
            def _():
                s_copy(first, 3 * me_c - 3, 2, h).start()

    @pl.when(odd == 1)
    def _():
        for copy in swaps:
            copy.wait_recv()

    target_block = lax.broadcasted_iota(jnp.int32, mask.shape, 1) // BS
    hit = jnp.zeros(mask.shape, jnp.float32)
    diagonal = (lax.broadcasted_iota(jnp.int32, (blocks, blocks), 0)
                == lax.broadcasted_iota(jnp.int32, (blocks, blocks), 1))

    def as_column(row):
        return jnp.sum(jnp.where(diagonal, row.astype(jnp.float32), 0.0), axis=1, keepdims=True)

    counts = as_column(count_ref[...])
    for k in range(slots):
        named = as_column(cand_ref[k:k + 1, :]).astype(jnp.int32)
        live = (named == target_block) & (counts > k)
        hit = jnp.where(live, 1.0, hit)
    mask[...] = hit

    ones = jnp.ones((16, T), jnp.bfloat16)
    scale = math.log2(math.e) / strength

    def tile(owner, b, t):
        block = sp[owner, b * BS:(b + 1) * BS, :]
        row0 = pl.multiple_of(owner * m + b * BS, BS)
        columns = pl.ds(pl.multiple_of(t * m, m), m)
        sim = lax.dot_general(block, tp[t], NT, preferred_element_type=jnp.float32)
        live = mask[pl.ds(owner * mb + b, 1), columns]
        gibbs[pl.ds(row0, BS), columns] = (jnp.exp2(sim * scale) * live).astype(jnp.bfloat16)

    def row_total(owner, b):
        rows = pl.ds(pl.multiple_of(owner * m + b * BS, BS), BS)
        total = lax.dot_general(ones, gibbs[rows, :], NT, preferred_element_type=jnp.float32)
        rbuf[0, me_c, :, rows] = total[:1]

    def build(owner):
        for b in range(mb):
            s_arrive(owner, b)
            for t in range(n_r):
                tile(owner, b, t)
            row_total(owner, b)

    here = (me_c, first) if relayed else (me_c,)
    near_row = 3 - 2 * lax.rem(me_r, 2) if n_r == 4 else 1
    for k in (0, near_row, 4 - near_row, 2) if n_r == 4 else range(n_r):
        t = lax.rem(me_r + n_r - k, n_r)
        if not (isinstance(k, int) and k == 0):
            row_copy(tp.at[t], t_send.at[k - 1], t_recv.at[k - 1], k).wait_recv()
        for owner in here:
            for b in range(mb):
                tile(owner, b, t)
    for owner in here:
        for b in range(mb):
            row_total(owner, b)
    if relayed:
        build(3 * lax.rem(me_c + 1, 2))
        build(to_col(2))
    else:
        def arrive(k, carry):
            build(to_col(k))
            return carry

        lax.fori_loop(1, n_c, arrive, 0)

    def chunked(extent):
        step = min(extent, 1024)
        return [slice(i, i + step) for i in range(0, extent, step)]

    def exchange_rows(it):
        out = [col_copy(rbuf.at[it, me_c], rbuf.at[it, me_c],
                        r_send.at[it, k - 1], r_recv.at[it, k - 1], k, role)
               for k in range(1, n_c)]
        for copy in out:
            copy.start()
        if it == 0:
            for k in range(1, n_c):
                from_col(lambda o: sm.at[o], sm_send.at[k - 1], sm_recv.at[k - 1], k)
        for k in range(1, n_c):
            from_col(lambda o: rbuf.at[it, o], r_send.at[it, k - 1], r_recv.at[it, k - 1], k)
        total = rbuf[it, 0]
        for j in range(1, n_c):
            total = total + rbuf[it, j]
        return out, jnp.concatenate([sm[j] for j in range(n_c)], axis=1) / total

    pending = t_out + sm_out + tm_out
    home = swap(4, pout, pin)

    def source_side():
        own = pl.ds(pl.multiple_of(me_c * m, m), m)
        total = rbuf[ITERS - 1, 0, :, own]
        for j in range(1, n_c):
            total = total + rbuf[ITERS - 1, j, :, own]
        pout[...] = strength * jnp.log(sm[me_c] / total)

        @pl.when(odd == 1)
        def _():
            home.start()
            for copy in swaps:
                copy.wait_send()

        for copy in pending:
            copy.wait_send()
        for k in range(1, n_c):
            for h in range(mb):
                own_copy(k, h).wait_send()

        @pl.when(odd == 1)
        def _():
            home.wait()
            pot_ref[0:1] = pin[...]

        @pl.when(odd == 0)
        def _():
            pot_ref[0:1] = pout[...]

    def exchange_cols(it):
        final = it == ITERS - 1

        def sums(o, reader):
            if not final:
                return cbuf.at[it, o]
            return cbuf.at[it, o, :, pl.ds(pl.multiple_of(reader * m, m), m)]

        out = [row_copy(sums(me_r, to_row(k)), c_send.at[it, k - 1], c_recv.at[it, k - 1], k)
               for k in range(1, n_r)]
        for copy in out:
            copy.start()
        if it == ITERS - 1:
            source_side()
        if it == 0:
            for k in range(1, n_r):
                from_row(lambda o: tm.at[o], tm_send.at[k - 1], tm_recv.at[k - 1], k)
        for k in range(1, n_r):
            from_row(lambda o: sums(o, me_r), c_send.at[it, k - 1], c_recv.at[it, k - 1], k)
        if final:
            return out, None
        total = cbuf[it, 0]
        for j in range(1, n_r):
            total = total + cbuf[it, j]
        return out, jnp.concatenate([tm[j] for j in range(n_r)], axis=1) / total

    for it in range(ITERS):
        if it > 0:
            rows = split_rows(v)
            for part in chunked(S):
                total = lax.dot_general(rows, gibbs[part, :], NT, preferred_element_type=jnp.float32)
                rbuf[it, me_c, :, part] = jnp.sum(total, axis=0, keepdims=True)
        out, u = exchange_rows(it)
        pending += out
        rows = split_rows(u)
        for part in chunked(T):
            total = lax.dot_general(rows, gibbs[:, part], NN, preferred_element_type=jnp.float32)
            cbuf[it, me_r, :, part] = jnp.sum(total, axis=0, keepdims=True)
        out, v = exchange_cols(it)
        if it < ITERS - 1:
            pending += out

    last = ITERS - 1
    own = pl.ds(pl.multiple_of(me_r * m, m), m)
    total = cbuf[last, 0, :, own]
    for j in range(1, n_r):
        total = total + cbuf[last, j, :, own]
    pot_ref[1:2] = strength * jnp.log(tm[me_r] / total)
    for copy in out:
        copy.wait_send()


def per_device(source_emb, target_emb, source_mass, target_mass, cand_cols, cand_count):
    n_r, n_c = lax.axis_size("rows"), lax.axis_size("cols")
    m, w = source_emb.shape
    S, T = n_c * m, n_r * m
    vmem = pl.BlockSpec(memory_space=pltpu.VMEM)
    dma = pltpu.SemaphoreType.DMA
    slots, blocks = cand_cols.shape[1], cand_cols.shape[0]
    pots = pl.pallas_call(
        functools.partial(kernel, n_r, n_c),
        out_shape=jax.ShapeDtypeStruct((2, m), jnp.float32),
        in_specs=[pl.BlockSpec(memory_space=pltpu.HBM)] * 6,
        out_specs=vmem,
        scratch_shapes=[
            pltpu.VMEM((m, w), jnp.bfloat16),
            pltpu.VMEM((m, w), jnp.bfloat16),
            pltpu.VMEM((1, m), jnp.float32),
            pltpu.VMEM((slots, blocks), jnp.int32),
            pltpu.VMEM((1, blocks), jnp.int32),
            pltpu.VMEM((slots, blocks), jnp.int32),
            pltpu.VMEM((1, blocks), jnp.int32),
            pltpu.VMEM((1, m), jnp.float32),
            pltpu.VMEM((1, m), jnp.float32),
            dma((6,)), dma((5,)), dma((5,)),
            pltpu.VMEM((n_c, m, w), jnp.bfloat16),
            pltpu.VMEM((n_r, m, w), jnp.bfloat16),
            pltpu.VMEM((n_c, 1, m), jnp.float32),
            pltpu.VMEM((n_r, 1, m), jnp.float32),
            pltpu.VMEM((blocks, T), jnp.float32),
            pltpu.VMEM((S, T), jnp.bfloat16),
            pltpu.VMEM((ITERS, n_c, 1, S), jnp.float32),
            pltpu.VMEM((ITERS, n_r, 1, T), jnp.float32),
            dma((n_c - 1, m // BS)), dma((n_c - 1, m // BS)),
            dma((n_r - 1,)), dma((n_r - 1,)),
            dma((n_c - 1,)), dma((n_c - 1,)), dma((n_r - 1,)), dma((n_r - 1,)),
            dma((ITERS, n_c - 1)), dma((ITERS, n_c - 1)),
            dma((ITERS, n_r - 1)), dma((ITERS, n_r - 1)),
        ],
        compiler_params=pltpu.CompilerParams(
            collective_id=0, has_side_effects=True,
            vmem_limit_bytes=63 << 20,
        ),
        name="sinkhorn",
    )(source_emb, target_emb, source_mass.reshape(1, m), target_mass.reshape(1, m),
      cand_cols.T, cand_count.T)
    return pots[0], pots[1]


def solution(mesh):
    placed = (
        P(("groups", "rows", "cols"), None),
        P(("groups", "cols", "rows"), None),
        P(("groups", "rows", "cols")),
        P(("groups", "cols", "rows")),
        P(("groups", "rows"), "cols"),
        P(("groups", "rows"), "cols"),
    )
    return jax.shard_map(
        per_device,
        mesh=mesh,
        in_specs=placed,
        out_specs=(P(("groups", "rows", "cols")), P(("groups", "cols", "rows"))),
        check_vma=False,
    )
```
